32 devices in a mesh: groups: 2 (over y), seq: 4 (over z), mp: 2 (over x), rep: 2 (over core).
Axes of the slice: x: 2, y: 2, z: 4, core: 2. Of those that a mesh axis runs over, the one named last changes fastest.
Arguments:
- tokens: bfloat16 [4, 2048, 1024], P(('groups', 'rep'), ('seq', 'mp')), parts along dimension 0, may hold values from -6 to 6
- w_qkv: bfloat16 [1024, 3, 1024], P(None, None, 'mp')
- w_attn_out: bfloat16 [1024, 1024], P('mp'), may hold values from -0.1875 to 0.1875
- w_in: bfloat16 [1024, 2624], P(None, 'mp'), may hold values from -0.1875 to 0.1875
- w_gate: bfloat16 [1024, 2624], P(None, 'mp'), may hold values from -0.1875 to 0.1875
- w_down: bfloat16 [1024, 2624], P(None, 'mp'), may hold values from -0.125 to 0.125
- w_colbert: bfloat16 [1024, 128], replicated, may hold values from -0.1875 to 0.1875
- gain_attn: float32 [1024], replicated, may hold values from 0.1 to 1.9
- gain_mlp: float32 [1024], replicated, may hold values from 0.1 to 1.9
- gain_final: float32 [1024], replicated, may hold values from 0.1 to 1.9
- lengths: int32 [4, 8], P(('groups', 'rep')), parts along dimension 0, may hold values from 1 to 1024, 2048 in all within a row
- owners: int32 [4, 2048, 1], P(('groups', 'rep'), ('seq', 'mp')), parts along dimension 0, may hold values from 0 to 15; in each aligned block of 256 rows (0 to 255, 256 to 511, ..., all dimensions but the last counted through in order) at most 32 rows name the same one
Outputs:
- routed: bfloat16 [512, 32, 128], P(('groups', 'seq', 'mp', 'rep')), parts along dimension 0
The draws below stay inside these ranges and needn't reach their ends.
There are 2 independent parts, one for each index of `groups`. The reference program is written for one: setup_inputs(seed, part) draws one part's arguments, and reference() takes and returns one part's arrays. A program takes and returns all parts, laid end to end along the dimension named above; an argument that names none is the same for every part. Nothing has to cross between parts.
Inputs may be any that keep to these rules, and one draw needn't show every extreme that they name: The 8 lengths of a slab sum to 2048 and the longest is exactly 1024. `owners`: within the 256 positions of one device (aligned blocks of the slab-major order) no owner appears more than 32 times; in every draw some owner appears exactly 32 times in some block.
All inputs are finite; a program needn't handle non-finite values.
Results may differ from the reference program's by a relative error of at most 0.01.
Values may be sent and summed in bfloat16 or wider, within the bound.
A program may use at most 128 MiB of HBM per device.

```python
import math
import jax
import jax.numpy as jnp
import numpy as np
from jax import lax

D = 1024
HEADS = 16
HEAD_DIM = 64
FF = 2624
DC = 128
WIN = 64
DOCS = 8
TOK_DEV = 256
HD = 1024
SLABS = 2
SLAB_LEN = 2048
MAXLEN = 1024
NOWN = 16
CAP = 32


def draw_w_qkv(key, part):
    key = jax.random.fold_in(key, 7)
    base_draw = jax.random.normal(key, (D, 3, HEADS * HEAD_DIM), jnp.float32) * D ** (-0.5)
    return base_draw.astype(jnp.bfloat16)


def levels(rng, dims, pieces, low, largest):
    factor_of, own = 1.0, jax.random.fold_in(rng, 6)
    for axis_at, blocks in pieces:
        steps = jnp.exp(jax.random.uniform(jax.random.fold_in(own, axis_at), (blocks,), jnp.float32, low / len(pieces), largest / len(pieces)))
        factor_of = factor_of * jnp.repeat(steps, dims[axis_at] // blocks).reshape([-1 if axis == axis_at else 1 for axis in range(len(dims))])
    return factor_of


def profile(amount, total, most, slope):
    portions = [(1 << 20) // math.isqrt(standing ** slope) + 1 for standing in range(2, amount + 1)]
    rest, given = total - most - (amount - 1), [1] * (amount - 1)
    while rest > 0:
        candidates = [i for i in range(amount - 1) if given[i] < most]
        whole, remaining = sum([portions[i] for i in candidates]), rest
        for i in candidates:
            more = min(most - given[i], max(1, remaining * portions[i] // whole), rest)
            given[i] = given[i] + more
            rest = rest - more
    return np.array([most] + given)


def uneven_parts(stream_key, amount, total, most, lean):
    if amount == 2:
        one = jax.random.randint(stream_key, (), max(1, total - most), min(most, total - 1) + 1)
        return jnp.stack([one, total - one])
    sizes = jnp.asarray(profile(amount, total, most, lean), jnp.int32)
    pairs = (amount - 1) // 2
    source_of, taker = sizes[1:1 + 2 * pairs:2], sizes[2:2 + 2 * pairs:2]
    slack = jnp.minimum(source_of - 1, most - taker)
    passed = jax.random.randint(jax.random.fold_in(stream_key, 1), (pairs,), 0, 1 << 20) % (slack + 1)
    sizes = sizes.at[1:1 + 2 * pairs:2].set(source_of - passed).at[2:2 + 2 * pairs:2].set(taker + passed)
    return sizes[jax.random.permutation(jax.random.fold_in(stream_key, 2), amount)]


def shared_out(key, own, number, rows, number_of, top, limit, lean):
    sequence = jax.random.permutation(key, number_of)
    heavy_load, common = shares(number_of, rows * top, limit, lean, True), shares(number_of, rows * top, limit, lean, False)
    places = jnp.arange(number_of)

    def named(tallies, turn):
        used = int((tallies > 0).sum())
        fixed = max(1, used // 4)
        shifted = fixed + (places - fixed + turn * (used - fixed)) % max(1, number_of - fixed)
        return jnp.zeros((number_of,), jnp.int32).at[sequence[jnp.where(places < fixed, places, shifted)]].set(jnp.asarray(tallies, jnp.int32))

    tallies = jnp.where(number % 4 == 0, named(heavy_load, number // 4), named(common, number - number // 4 - 1))
    mixed = jax.random.permutation(jax.random.fold_in(own, 3), number_of)
    source_of, sink = mixed[0:number_of // 2 * 2:2], mixed[1:number_of // 2 * 2:2]
    room = jnp.minimum(tallies[source_of] - 1, limit - tallies[sink]) // 2
    room = jnp.where((source_of == sequence[0]) | (sink == sequence[0]) | (tallies[sink] == 0), 0, jnp.maximum(room, 0))
    shifted = jax.random.randint(jax.random.fold_in(own, 4), (number_of // 2,), 0, 1 << 20) % (room + 1)
    tallies = tallies.at[source_of].add(-shifted).at[sink].add(shifted)
    labels = jnp.searchsorted(jnp.cumsum(tallies), jnp.arange(rows * top), side="right").astype(jnp.int32)
    grid = labels.reshape(top, rows).T
    grid = grid[jax.random.permutation(jax.random.fold_in(own, 1), rows)]
    turn = jax.random.randint(jax.random.fold_in(own, 2), (rows, 1), 0, top)
    return jnp.take_along_axis(grid, (jnp.arange(top)[None, :] + turn) % top, axis=1)


def shares(number_of, total, most, lean, full):
    portions = [(1 << 20) // math.isqrt(standing ** lean) + 1 for standing in range(1, number_of + 1)]
    largest = most if full else min(most, max(-(-total // number_of), total * portions[0] // sum(portions)))
    least = 1 if total - largest >= number_of - 1 else 0
    given, rest = [largest] + [least] * (number_of - 1), total - largest - least * (number_of - 1)
    while rest > 0:
        candidates = [i for i in range(1, number_of) if given[i] < largest] or [i for i in range(1, number_of) if given[i] < most]
        whole, budget = sum([portions[i] for i in candidates]), rest
        for i in candidates:
            extra = min(most - given[i], max(1, budget * portions[i] // whole), rest)
            given[i] = given[i] + extra
            rest = rest - extra
    return np.array(given)


def scatter_about(stream_key, dims, deviation, most, cuts=(), kind=jnp.bfloat16):
    level = levels(stream_key, dims, cuts, -0.22, 0.18) if cuts else 1.0
    drawn = jax.random.normal(stream_key, dims, jnp.float32) * deviation * level
    return jnp.minimum(jnp.maximum(drawn, -most), most).astype(kind)


def setup_inputs(seed: int = 0, part: int = 0) -> dict:
    arg_keys = jax.random.split(jax.random.key(seed), 13)
    own_keys = jax.random.split(jax.random.fold_in(arg_keys[12], part), 13)
    tokens = scatter_about(own_keys[0], (SLABS, SLAB_LEN, D), 1.0, 6.0, ((0, 2), (1, 8)))
    w_qkv = draw_w_qkv(jax.random.fold_in(arg_keys[12], 71), part)
    w_attn_out = scatter_about(arg_keys[2], (HD, D), HD ** -0.5, 0.1875, ((0, 2),))
    w_in = scatter_about(arg_keys[3], (D, FF), D ** -0.5, 0.1875, ((1, 2),))
    w_gate = scatter_about(arg_keys[4], (D, FF), D ** -0.5, 0.1875, ((1, 2),))
    w_down = scatter_about(arg_keys[5], (D, FF), FF ** -0.5, 0.125, ((1, 2),))
    w_colbert = scatter_about(arg_keys[6], (D, DC), D ** -0.5, 0.1875)
    gain_attn = jnp.clip(1.0 + 0.18 * jax.random.normal(arg_keys[7], (D,), jnp.float32), 0.1, 1.9)
    gain_mlp = jnp.clip(1.0 + 0.18 * jax.random.normal(arg_keys[8], (D,), jnp.float32), 0.1, 1.9)
    gain_final = jnp.clip(1.0 + 0.18 * jax.random.normal(arg_keys[9], (D,), jnp.float32), 0.1, 1.9)
    lengths = jax.vmap(lambda own: uneven_parts(own, DOCS, SLAB_LEN, MAXLEN, 2))(jax.random.split(own_keys[10], SLABS)).reshape((SLABS, DOCS)).astype(jnp.int32)
    owners_keys = jax.random.split(jax.random.fold_in(own_keys[11], 1), SLABS * SLAB_LEN // TOK_DEV)
    owners_turns = jax.random.permutation(jax.random.fold_in(own_keys[11], 3), SLABS * SLAB_LEN // TOK_DEV)
    owners = jax.vmap(lambda own, number: shared_out(jax.random.fold_in(own_keys[11], 2), own, number, TOK_DEV, NOWN, 1, CAP, 2))(owners_keys, owners_turns).reshape((SLABS, SLAB_LEN, 1))
    return dict(tokens=tokens, w_qkv=w_qkv, w_attn_out=w_attn_out, w_in=w_in, w_gate=w_gate, w_down=w_down, w_colbert=w_colbert, gain_attn=gain_attn, gain_mlp=gain_mlp, gain_final=gain_final, lengths=lengths, owners=owners)


epsilon = 1e-05
rope_base = 10000.0

def layer_norm(values, norm_gain):
    average = lax.optimization_barrier(jnp.mean(values, axis=-1, keepdims=True))
    centered = values - average
    spread = lax.optimization_barrier(jnp.mean(centered * centered, axis=-1, keepdims=True))
    return centered * lax.rsqrt(spread + epsilon) * norm_gain

def doc_layout(doc_lengths, first_row, row_total):
    doc_ends = jnp.cumsum(doc_lengths)
    doc_starts = doc_ends - doc_lengths
    doc_total = doc_ends[-1]
    position = first_row + jnp.arange(row_total, dtype=jnp.int32)
    started = doc_starts[None, :] <= position[:, None]
    doc_id = lax.optimization_barrier(jnp.sum(started.astype(jnp.int32), axis=1)) - 1
    start_of = lax.optimization_barrier(jnp.max(jnp.where(started, doc_starts[None, :], 0), axis=1))
    inside = (position >= 0) & (position < doc_total)
    return (jnp.where(inside, doc_id, -1), position - start_of)

def rotate(values, offsets):
    half_dim = HEAD_DIM // 2
    row_count = values.shape[0]
    head_count = values.shape[1] // HEAD_DIM
    frequency = rope_base ** (-(jnp.arange(half_dim, dtype=jnp.float32) * 2.0) / HEAD_DIM)
    angles = offsets.astype(jnp.float32)[:, None] * frequency[None, :]
    cosine = jnp.cos(angles)[:, None, :]
    sine_part = jnp.sin(angles)[:, None, :]
    shaped = values.reshape(row_count, head_count, HEAD_DIM)
    first_half = shaped[..., :half_dim]
    second_half = shaped[..., half_dim:]
    turned = jnp.concatenate([first_half * cosine - second_half * sine_part, second_half * cosine + first_half * sine_part], axis=-1)
    return turned.reshape(row_count, head_count * HEAD_DIM)

def window_attention(queries, key_rows, value_rows, query_docs, key_docs):
    row_count = queries.shape[0]
    head_count = queries.shape[1] // HEAD_DIM
    block_rows = min(512, row_count)
    key_span = block_rows + 2 * WIN
    outputs = []
    for block_index in range(row_count // block_rows):
        block_low = block_index * block_rows
        query_block = queries[block_low:block_low + block_rows].reshape(block_rows, head_count, HEAD_DIM).astype(jnp.float32)
        key_block = key_rows[block_low:block_low + key_span].reshape(key_span, head_count, HEAD_DIM).astype(jnp.float32)
        value_block = value_rows[block_low:block_low + key_span].reshape(key_span, head_count, HEAD_DIM).astype(jnp.float32)
        scores = jnp.einsum('qhd,khd->hqk', query_block, key_block) * HEAD_DIM ** (-0.5)
        key_lag = jnp.arange(key_span)[None, :] - jnp.arange(block_rows)[:, None]
        allowed = (key_lag >= 0) & (key_lag <= 2 * WIN) & (query_docs[block_low:block_low + block_rows, None] == key_docs[None, block_low:block_low + key_span])
        scores = jnp.where(allowed[None], scores, -jnp.inf)
        row_max = lax.optimization_barrier(jnp.max(scores, axis=2, keepdims=True))
        weights = jnp.exp(scores - row_max)
        probabilities = (weights / lax.optimization_barrier(jnp.sum(weights, axis=2, keepdims=True))).astype(jnp.bfloat16)
        mixed = jnp.einsum('hqk,khd->qhd', probabilities.astype(jnp.float32), value_block)
        outputs.append(mixed.reshape(block_rows, head_count * HEAD_DIM))
    return jnp.concatenate(outputs, axis=0).astype(jnp.bfloat16)

def reference(tokens, w_qkv, w_attn_out, w_in, w_gate, w_down, w_colbert, gain_attn, gain_mlp, gain_final, lengths, owners):
    slab_vectors = []
    for slab_index in range(SLABS):
        local_tokens = tokens[slab_index].astype(jnp.float32)
        normed = layer_norm(local_tokens, gain_attn).astype(jnp.bfloat16)
        projected = jnp.dot(normed, w_qkv.reshape(D, 3 * HD), preferred_element_type=jnp.float32)
        query_docs, offsets = doc_layout(lengths[slab_index], 0, SLAB_LEN)
        key_docs, _ = doc_layout(lengths[slab_index], -WIN, SLAB_LEN + 2 * WIN)
        queries = rotate(projected[:, :HD], offsets).astype(jnp.bfloat16)
        key_rows = rotate(projected[:, HD:2 * HD], offsets).astype(jnp.bfloat16)
        value_rows = projected[:, 2 * HD:].astype(jnp.bfloat16)
        margin = jnp.zeros((WIN, HD), jnp.bfloat16)
        key_rows = jnp.concatenate([margin, key_rows, margin], axis=0)
        value_rows = jnp.concatenate([margin, value_rows, margin], axis=0)
        context = window_attention(queries, key_rows, value_rows, query_docs, key_docs)
        mixed = local_tokens + jnp.dot(context, w_attn_out, preferred_element_type=jnp.float32)
        mlp_normed = layer_norm(mixed, gain_mlp).astype(jnp.bfloat16)
        gate_in = jnp.dot(mlp_normed, w_in, preferred_element_type=jnp.float32)
        gate_side = jnp.dot(mlp_normed, w_gate, preferred_element_type=jnp.float32)
        hidden = (jax.nn.gelu(gate_in, approximate=False) * gate_side).astype(jnp.bfloat16)
        result = mixed + lax.dot_general(hidden, w_down, (((1,), (1,)), ((), ())), preferred_element_type=jnp.float32)
        final_normed = layer_norm(result, gain_final).astype(jnp.bfloat16)
        colbert_raw = jnp.dot(final_normed, w_colbert, preferred_element_type=jnp.float32)
        vectors = (colbert_raw * lax.rsqrt(lax.optimization_barrier(jnp.mean(colbert_raw * colbert_raw, axis=1, keepdims=True)) + 1e-06)).astype(jnp.bfloat16)
        slab_vectors.append(vectors)
    vectors = jnp.stack(slab_vectors)
    block_count = SLAB_LEN // TOK_DEV
    owner_grid = owners[:, :, 0].reshape(SLABS, block_count, TOK_DEV)
    chosen = (owner_grid[..., None] == jnp.arange(NOWN, dtype=jnp.int32)).astype(jnp.int32)
    slot_rank = lax.optimization_barrier(jnp.sum(jnp.cumsum(chosen, axis=2) * chosen, axis=3)) - 1
    source = jnp.arange(block_count, dtype=jnp.int32)[None, :, None] * SLABS + jnp.arange(SLABS, dtype=jnp.int32)[:, None, None]
    target = ((owner_grid * NOWN + source) * CAP + slot_rank).reshape(-1).astype(jnp.int32)
    routed = jnp.zeros((NOWN * NOWN * CAP, DC), jnp.bfloat16).at[target].set(vectors.reshape(-1, DC))
    return routed.reshape(NOWN * NOWN, CAP, DC)
```

```python
import functools

import jax
import jax.numpy as jnp
from jax import lax
from jax.experimental import pallas as pl
from jax.experimental.pallas import tpu as pltpu
from jax.sharding import PartitionSpec as P

HEAD_DIM = 64
WIN = 64
LANES = 128
MESH = pl.DeviceIdType.MESH
EPS = 1e-05
LOG_BASE = 9.210340371976184

CHUNK = 64
BLOCK = 128
COLS = 256

f32 = jnp.float32
bf16 = jnp.bfloat16


def layer_norm(values, gain):
    average = jnp.mean(values, axis=-1, keepdims=True)
    centered = values - average
    spread = jnp.mean(centered * centered, axis=-1, keepdims=True)
    return centered * lax.rsqrt(spread + EPS) * gain


def dot(a, b):
    return jnp.dot(a, b, preferred_element_type=f32)


def dot_nt(a, b):
    return lax.dot_general(a, b, (((1,), (1,)), ((), ())), preferred_element_type=f32)


def layer_kernel(
    sizes,
    lengths,
    tokens,
    owner_row,
    gain_attn,
    gain_mlp,
    gain_final,
    w_colbert,
    w_qkv_hbm,
    w_out_hbm,
    w_in_hbm,
    w_gate_hbm,
    w_down_hbm,
    out,
    w_qkv,
    w_out,
    w_in,
    w_gate,
    w_down,
    xn,
    xn2,
    qkv,
    edge,
    cosine,
    sine,
    disp,
    mixed,
    total,
    rs1s,
    rs1r,
    rs2s,
    rs2r,
    ctx,
    hid,
    vec,
    outb,
    w_sem,
    ag1_s,
    ag1_r,
    halo_s,
    halo_r,
    rs1_ss,
    rs1_rs,
    ag2_s,
    ag2_r,
    rs2_ss,
    rs2_rs,
    a2a_s,
    a2a_r,
    own_sem,
):
    seqs, mps, reps = sizes
    peers = seqs * mps * reps
    rows = tokens.shape[0]
    span = rows * mps
    inner = w_out.shape[0]
    pairs = inner // LANES
    hidden = w_in.shape[0]
    slots = out.shape[1]
    chunks = rows // CHUNK
    blocks = rows // BLOCK

    seq = lax.axis_index("seq")
    mp = lax.axis_index("mp")
    rep = lax.axis_index("rep")
    me = (seq * mps + mp) * reps + rep
    first_row = seq * span

    def device(p):
        return {
            "seq": lax.div(p, mps * reps),
            "mp": lax.rem(lax.div(p, reps), mps),
            "rep": lax.rem(p, reps),
        }

    weights = [
        pltpu.make_async_copy(src, dst, w_sem.at[i])
        for i, (src, dst) in enumerate(
            [
                (w_qkv_hbm, w_qkv),
                (w_out_hbm, w_out),
                (w_in_hbm, w_in),
                (w_gate_hbm, w_gate),
                (w_down_hbm, w_down),
            ]
        )
    ]
    for copy in weights:
        copy.start()

    barrier = pltpu.get_barrier_semaphore()

    @pl.loop(1, peers)
    def _(k):
        pl.semaphore_signal(
            barrier, inc=1, device_id=device(lax.rem(me + k, peers)), device_id_type=MESH
        )

    def mp_copy(src, dst, send, recv, k):
        return pltpu.make_async_remote_copy(
            src_ref=src,
            dst_ref=dst,
            send_sem=send,
            recv_sem=recv,
            device_id={"mp": lax.rem(mp + k, mps)},
            device_id_type=MESH,
        )

    def chunk_row(owner, c):
        last = lax.div(owner, mps - 1)
        return pl.multiple_of((c + last * (chunks - 1 - 2 * c)) * CHUNK, CHUNK)

    def ag1(owner, c, k):
        at = pl.ds(pl.multiple_of(owner * rows + chunk_row(owner, c), CHUNK), CHUNK)
        return mp_copy(xn.at[at], xn.at[at], ag1_s.at[k - 1, c], ag1_r.at[k - 1, c], k)

    for c in range(chunks):
        at = chunk_row(mp, c)
        part = layer_norm(tokens[pl.ds(at, CHUNK), :].astype(f32), gain_attn[...])
        xn[pl.ds(pl.multiple_of(mp * rows + at, CHUNK), CHUNK), :] = part.astype(bf16)
        if c == 0:
            pl.semaphore_wait(barrier, peers - 1)
        for k in range(1, mps):
            ag1(mp, c, k).start()

    docs = lengths.shape[1]
    starts = [jnp.int32(0)]
    for d in range(docs):
        starts.append(starts[-1] + lengths[0, d])

    def doc_bounds(position):
        low = jnp.zeros_like(position)
        high = jnp.zeros_like(position) + starts[1]
        for d in range(1, docs):
            inside = position >= starts[d]
            low = jnp.where(inside, starts[d], low)
            high = jnp.where(inside, starts[d + 1], high)
        return low, high

    lane = lax.broadcasted_iota(jnp.int32, (1, LANES), 1)
    first_half = lax.rem(lane, HEAD_DIM) < HEAD_DIM // 2
    frequency = jnp.exp(
        lax.rem(lane, HEAD_DIM // 2).astype(f32) * (-2.0 * LOG_BASE / HEAD_DIM)
    )

    @pl.loop(0, span // CHUNK)
    def _(i):
        at = pl.ds(pl.multiple_of(i * CHUNK, CHUNK), CHUNK)
        position = first_row + i * CHUNK + lax.broadcasted_iota(jnp.int32, (CHUNK, 1), 0)
        offset = position - doc_bounds(position)[0]
        angle = offset.astype(f32) * frequency
        cosine[at, :] = jnp.cos(angle)
        turned = jnp.sin(angle)
        sine[at, :] = jnp.where(first_half, -turned, turned)

    def rotate(values, c, s):
        swapped = jnp.where(
            first_half,
            pltpu.roll(values, LANES - HEAD_DIM // 2, 1),
            pltpu.roll(values, HEAD_DIM // 2, 1),
        )
        return values * c + swapped * s

    weights[0].wait()

    def project(x, part, c, s, put):
        for low in range(0, inner, COLS):
            y = dot(x, w_qkv[part, :, low : low + COLS])
            for half in range(0, COLS, LANES):
                piece = y[:, half : half + LANES]
                if part < 2:
                    piece = rotate(piece, c, s)
                if part == 0:
                    piece = piece * HEAD_DIM**-0.5
                put(low + half, piece.astype(bf16))

    for k in range(1, mps):
        ag1(lax.rem(mp + mps - k, mps), 0, k).wait_recv()
    top = span - WIN
    x_edge = jnp.concatenate([xn[0:WIN, :], xn[top:span, :]], axis=0)
    c_edge = jnp.concatenate([cosine[0:WIN, :], cosine[top:span, :]], axis=0)
    s_edge = jnp.concatenate([sine[0:WIN, :], sine[top:span, :]], axis=0)
    for part in (1, 2):

        def put_edge(col, piece, base=(part - 1) * inner):
            edge[:, base + col : base + col + LANES] = piece

        project(x_edge, part, c_edge, s_edge, put_edge)

    def halo(side):
        src = edge.at[pl.ds(side * WIN, WIN), :]
        dst = qkv.at[pl.ds((WIN + span) * (1 - side), WIN), pl.ds(inner, 2 * inner)]
        to = lax.rem(seq + (seqs - 1 if side == 0 else 1), seqs)
        return pltpu.make_async_remote_copy(
            src_ref=src,
            dst_ref=dst,
            send_sem=halo_s.at[side],
            recv_sem=halo_r.at[side],
            device_id={"seq": to},
            device_id_type=MESH,
        )

    @pl.when(seq > 0)
    def _():
        halo(0).start()

    @pl.when(seq < seqs - 1)
    def _():
        halo(1).start()

    @pl.when(seq == 0)
    def _():
        qkv[0:WIN, inner:] = jnp.zeros((WIN, 2 * inner), bf16)

    @pl.when(seq == seqs - 1)
    def _():
        qkv[WIN + span :, inner:] = jnp.zeros((WIN, 2 * inner), bf16)

    @pl.loop(0, mps)
    def _(i):
        owner = lax.rem(mp + mps - i, mps)

        @pl.when(i > 0)
        def _():
            for c in range(1, chunks):
                at = pl.ds(pl.multiple_of(owner * rows + chunk_row(owner, c), CHUNK), CHUNK)
                mp_copy(
                    xn.at[at], xn.at[at], ag1_s.at[i - 1, c], ag1_r.at[i - 1, c], i
                ).wait_recv()

        at = pl.multiple_of(owner * rows, rows)
        x = xn[pl.ds(at, rows), :]
        c, s = cosine[pl.ds(at, rows), :], sine[pl.ds(at, rows), :]
        for part in range(3):

            def put(col, piece, base=part * inner):
                qkv[pl.ds(pl.multiple_of(at + WIN, WIN), rows), base + col : base + col + LANES] = piece

            project(x, part, c, s, put)

    owner_of = owner_row[...]
    chosen = (owner_of == lax.broadcasted_iota(jnp.int32, (peers, rows), 0)).astype(f32)
    before = (
        lax.broadcasted_iota(jnp.int32, (rows, rows), 0)
        <= lax.broadcasted_iota(jnp.int32, (rows, rows), 1)
    ).astype(f32)
    running = dot(chosen.astype(bf16), before.astype(bf16))
    rank = jnp.sum(running * chosen, axis=0, keepdims=True) - 1.0
    target = owner_of.astype(f32) * slots + rank
    slot_id = lax.broadcasted_iota(jnp.int32, (peers * slots, rows), 0).astype(f32)
    disp[...] = (target == slot_id).astype(f32).astype(bf16)

    weights[1].wait()

    @pl.when(seq < seqs - 1)
    def _():
        halo(0).wait_recv()

    @pl.when(seq > 0)
    def _():
        halo(1).wait_recv()

    head_lane = lane < HEAD_DIM
    ones = jnp.ones((BLOCK + 2 * WIN, LANES), bf16)

    def attend(low):
        position = first_row + low + lax.broadcasted_iota(jnp.int32, (BLOCK, 1), 0)
        start, end = doc_bounds(position)
        start = jnp.maximum(start, position - WIN)
        end = jnp.minimum(end - 1, position + WIN)
        key = first_row + low - WIN + lax.broadcasted_iota(jnp.int32, (1, BLOCK + 2 * WIN), 1)
        allowed = (key >= start) & (key <= end)
        allowed = jnp.concatenate([allowed.astype(f32)] * 2, axis=0) > 0.5
        at_q = pl.ds(pl.multiple_of(low + WIN, WIN), BLOCK)
        at_k = pl.ds(pl.multiple_of(low, WIN), BLOCK + 2 * WIN)
        for pair in range(pairs):
            col = pair * LANES
            q = qkv[at_q, col : col + LANES].astype(f32)
            q = jnp.concatenate(
                [jnp.where(head_lane, q, 0.0), jnp.where(head_lane, 0.0, q)], axis=0
            ).astype(bf16)
            scores = dot_nt(q, qkv[at_k, inner + col : inner + col + LANES])
            scores = jnp.where(allowed, scores, -jnp.inf)
            weight = jnp.exp(scores - jnp.max(scores, axis=1, keepdims=True)).astype(bf16)
            v = qkv[at_k, 2 * inner + col : 2 * inner + col + LANES]
            o = dot(weight, jnp.concatenate([v, ones], axis=1))
            o = o[:, :LANES] / o[:, LANES:]
            ctx[:, col : col + LANES] = jnp.where(head_lane, o[:BLOCK], o[BLOCK:]).astype(bf16)
        return dot(ctx[...], w_out[...])

    def spread(buffer_s, buffer_r, send, recv, k, b):
        at = pl.ds(pl.multiple_of(b * BLOCK, BLOCK), BLOCK)
        return mp_copy(
            buffer_s.at[k - 1, at], buffer_r.at[k - 1, at], send.at[k - 1, b], recv.at[k - 1, b], k
        )

    @pl.loop(0, mps * blocks)
    def _(i):
        k = 1 + lax.rem(i, mps - 1) if mps > 2 else 1
        b = lax.div(i, mps - 1)
        is_own = i >= (mps - 1) * blocks
        own_b = i - (mps - 1) * blocks
        owner = jnp.where(is_own, mp, lax.rem(mp + k, mps))
        b = jnp.where(is_own, own_b, b)
        partial = attend(owner * rows + b * BLOCK)
        at = pl.ds(pl.multiple_of(b * BLOCK, BLOCK), BLOCK)

        @pl.when(is_own)
        def _():
            mixed[at, :] = partial + tokens[at, :].astype(f32)

        @pl.when(jnp.logical_not(is_own))
        def _():
            rs1s[k - 1, at, :] = partial.astype(bf16)
            spread(rs1s, rs1r, rs1_ss, rs1_rs, k, b).start()

    def ag2(owner, b, k):
        at = pl.ds(pl.multiple_of(owner * rows + b * BLOCK, BLOCK), BLOCK)
        return mp_copy(xn2.at[at], xn2.at[at], ag2_s.at[k - 1, b], ag2_r.at[k - 1, b], k)

    for b in range(blocks):
        at = slice(b * BLOCK, (b + 1) * BLOCK)
        value = mixed[at, :]
        for k in range(1, mps):
            spread(rs1s, rs1r, rs1_ss, rs1_rs, k, b).wait_recv()
            value = value + rs1r[k - 1, at, :].astype(f32)
        mixed[at, :] = value
        low = pl.multiple_of(mp * rows + b * BLOCK, BLOCK)
        xn2[pl.ds(low, BLOCK), :] = layer_norm(value, gain_mlp[...]).astype(bf16)
        for k in range(1, mps):
            ag2(mp, b, k).start()

    for copy in weights[2:]:
        copy.wait()

    def mlp(low):
        x = xn2[pl.ds(pl.multiple_of(low, BLOCK), BLOCK), :]
        for at in range(0, hidden, COLS):
            to = min(at + COLS, hidden)
            a = dot_nt(x, w_in[at:to, :])
            g = dot_nt(x, w_gate[at:to, :])
            a = 0.5 * a * (1.0 + lax.erf(a * (0.5**0.5)))
            hid[:, at:to] = (a * g).astype(bf16)
        return dot(hid[...], w_down[...])

    others = (mps - 1) * blocks

    @pl.loop(0, mps * blocks)
    def _(i):
        j = jnp.clip(i - 1, 0, others - 1)
        is_other = (i >= 1) & (i <= others)
        k = 1 + lax.rem(j, mps - 1) if mps > 2 else 1
        b = jnp.where(is_other, lax.div(j, mps - 1), jnp.maximum(i - others, 0))
        owner = jnp.where(is_other, lax.rem(mp + k, mps), mp)

        @pl.when(is_other)
        def _():
            back = mps - k
            at = pl.ds(pl.multiple_of(owner * rows + b * BLOCK, BLOCK), BLOCK)
            mp_copy(
                xn2.at[at], xn2.at[at], ag2_s.at[back - 1, b], ag2_r.at[back - 1, b], back
            ).wait_recv()

        partial = mlp(owner * rows + b * BLOCK)
        at = pl.ds(pl.multiple_of(b * BLOCK, BLOCK), BLOCK)

        @pl.when(is_other)
        def _():
            rs2s[k - 1, at, :] = partial.astype(bf16)
            spread(rs2s, rs2r, rs2_ss, rs2_rs, k, b).start()

        @pl.when(jnp.logical_not(is_other))
        def _():
            total[at, :] = partial + mixed[at, :]

    for b in range(blocks):
        at = slice(b * BLOCK, (b + 1) * BLOCK)
        value = total[at, :]
        for k in range(1, mps):
            spread(rs2s, rs2r, rs2_ss, rs2_rs, k, b).wait_recv()
            value = value + rs2r[k - 1, at, :].astype(f32)
        final = layer_norm(value, gain_final[...]).astype(bf16)
        raw = dot(final, w_colbert[...])
        vec[at, :] = (
            raw * lax.rsqrt(jnp.mean(raw * raw, axis=1, keepdims=True) + 1e-06)
        ).astype(bf16)

    routed = dot(disp[...], vec[...])
    for p in range(peers):
        outb[p] = routed[p * slots : (p + 1) * slots].astype(bf16)

    def a2a(to, source):
        return pltpu.make_async_remote_copy(
            src_ref=outb.at[to],
            dst_ref=out.at[source],
            send_sem=a2a_s.at[to],
            recv_sem=a2a_r.at[source],
            device_id=device(to),
            device_id_type=MESH,
        )

    @pl.loop(1, peers)
    def _(k):
        a2a(lax.rem(me + k, peers), me).start()

    own = pltpu.make_async_copy(outb.at[me], out.at[me], own_sem)
    own.start()

    for k in range(1, mps):
        for c in range(chunks):
            ag1(mp, c, k).wait_send()
        for b in range(blocks):
            spread(rs1s, rs1r, rs1_ss, rs1_rs, k, b).wait_send()
            ag2(mp, b, k).wait_send()
            spread(rs2s, rs2r, rs2_ss, rs2_rs, k, b).wait_send()

    @pl.when(seq > 0)
    def _():
        halo(0).wait_send()

    @pl.when(seq < seqs - 1)
    def _():
        halo(1).wait_send()

    own.wait()

    @pl.loop(1, peers)
    def _(k):
        other = lax.rem(me + k, peers)
        a2a(other, me).wait_send()
        a2a(other, other).wait_recv()


def per_device(
    sizes,
    tokens,
    w_qkv,
    w_attn_out,
    w_in,
    w_gate,
    w_down,
    w_colbert,
    gain_attn,
    gain_mlp,
    gain_final,
    lengths,
    owners,
):
    seqs, mps, reps = sizes
    rows, width = tokens.shape[1:]
    peers = seqs * mps * reps
    slots = max(2, 2 * rows // peers)
    inner = w_attn_out.shape[0]
    hidden = w_in.shape[1]
    span = rows * mps
    dc = w_colbert.shape[1]
    chunks, blocks = rows // CHUNK, rows // BLOCK
    vmem = pl.BlockSpec(memory_space=pltpu.VMEM)
    anywhere = pl.BlockSpec(memory_space=pl.ANY)
    dma = pltpu.SemaphoreType.DMA
    return pl.pallas_call(
        functools.partial(layer_kernel, sizes),
        out_shape=jax.ShapeDtypeStruct((peers, slots, dc), bf16),
        in_specs=[pl.BlockSpec(memory_space=pltpu.SMEM)] + [vmem] * 6 + [anywhere] * 5,
        out_specs=anywhere,
        scratch_shapes=[
            pltpu.VMEM((3, width, inner), bf16),
            pltpu.VMEM((inner, width), bf16),
            pltpu.VMEM((hidden, width), bf16),
            pltpu.VMEM((hidden, width), bf16),
            pltpu.VMEM((hidden, width), bf16),
            pltpu.VMEM((span, width), bf16),
            pltpu.VMEM((span, width), bf16),
            pltpu.VMEM((span + 2 * WIN, 3 * inner), bf16),
            pltpu.VMEM((2 * WIN, 2 * inner), bf16),
            pltpu.VMEM((span, LANES), f32),
            pltpu.VMEM((span, LANES), f32),
            pltpu.VMEM((peers * slots, rows), bf16),
            pltpu.VMEM((rows, width), f32),
            pltpu.VMEM((rows, width), f32),
            pltpu.VMEM((mps - 1, rows, width), bf16),
            pltpu.VMEM((mps - 1, rows, width), bf16),
            pltpu.VMEM((mps - 1, rows, width), bf16),
            pltpu.VMEM((mps - 1, rows, width), bf16),
            pltpu.VMEM((BLOCK, inner), bf16),
            pltpu.VMEM((BLOCK, hidden), bf16),
            pltpu.VMEM((rows, dc), bf16),
            pltpu.VMEM((peers, slots, dc), bf16),
            dma((5,)),
            dma((mps - 1, chunks)),
            dma((mps - 1, chunks)),
            dma((2,)),
            dma((2,)),
            dma((mps - 1, blocks)),
            dma((mps - 1, blocks)),
            dma((mps - 1, blocks)),
            dma((mps - 1, blocks)),
            dma((mps - 1, blocks)),
            dma((mps - 1, blocks)),
            dma((peers,)),
            dma((peers,)),
            dma,
        ],
        compiler_params=pltpu.CompilerParams(
            collective_id=0, has_side_effects=True, vmem_limit_bytes=48 * 1024 * 1024
        ),
    )(
        lengths,
        tokens[0],
        owners.reshape(1, rows),
        gain_attn.reshape(1, width),
        gain_mlp.reshape(1, width),
        gain_final.reshape(1, width),
        w_colbert,
        jnp.transpose(w_qkv, (1, 0, 2)),
        w_attn_out,
        w_in.T,
        w_gate.T,
        w_down.T,
    )


def solution(mesh):
    sizes = (mesh.shape["seq"], mesh.shape["mp"], mesh.shape["rep"])
    return jax.shard_map(
        functools.partial(per_device, sizes),
        mesh=mesh,
        in_specs=(
            P(("groups", "rep"), ("seq", "mp"), None),
            P(None, None, "mp"),
            P("mp", None),
            P(None, "mp"),
            P(None, "mp"),
            P(None, "mp"),
            P(),
            P(),
            P(),
            P(),
            P(("groups", "rep"), None),
            P(("groups", "rep"), ("seq", "mp"), None),
        ),
        out_specs=P(("groups", "seq", "mp", "rep"), None, None),
        check_vma=False,
    )
```

```python
import functools

import jax
import jax.numpy as jnp
from jax import lax
from jax.experimental import pallas as pl
from jax.experimental.pallas import tpu as pltpu
from jax.sharding import PartitionSpec as P

HEAD_DIM = 64
WIN = 64
LANES = 128
MESH = pl.DeviceIdType.MESH
EPS = 1e-05
LOG_BASE = 9.210340371976184

CHUNK = 64
BLOCK = 128
COLS = 256

f32 = jnp.float32
bf16 = jnp.bfloat16


def layer_norm(values, gain):
    average = jnp.mean(values, axis=-1, keepdims=True)
    centered = values - average
    spread = jnp.mean(centered * centered, axis=-1, keepdims=True)
    return centered * lax.rsqrt(spread + EPS) * gain


def dot(a, b):
    return jnp.dot(a, b, preferred_element_type=f32)


def dot_nt(a, b):
    return lax.dot_general(a, b, (((1,), (1,)), ((), ())), preferred_element_type=f32)


def layer_kernel(
    sizes,
    lengths_hbm,
    tokens_hbm,
    owner_row_hbm,
    gain_attn_hbm,
    gain_mlp_hbm,
    gain_final_hbm,
    w_colbert_hbm,
    w_qkv_hbm,
    w_out_hbm,
    w_in_hbm,
    w_gate_hbm,
    w_down_hbm,
    out,
    lengths,
    tokens,
    owner_row,
    gain_attn,
    gain_mlp,
    gain_final,
    w_colbert,
    w_qkv,
    w_out,
    w_in,
    w_gate,
    w_down,
    xn,
    xn2,
    qkv,
    edge,
    cosine,
    sine,
    disp,
    mixed,
    total,
    rs1s,
    rs1r,
    rs2s,
    rs2r,
    ctx,
    hid,
    vec,
    outb,
    w_sem,
    ag1_s,
    ag1_r,
    halo_s,
    halo_r,
    rs1_ss,
    rs1_rs,
    ag2_s,
    ag2_r,
    rs2_ss,
    rs2_rs,
    a2a_s,
    a2a_r,
    own_sem,
):
    seqs, mps, reps = sizes
    peers = seqs * mps * reps
    rows = tokens.shape[0]
    span = rows * mps
    inner = w_out.shape[0]
    pairs = inner // LANES
    hidden = w_in.shape[0]
    slots = out.shape[1]
    chunks = rows // CHUNK
    blocks = rows // BLOCK

    seq = lax.axis_index("seq")
    mp = lax.axis_index("mp")
    rep = lax.axis_index("rep")
    me = (seq * mps + mp) * reps + rep
    first_row = seq * span

    def device(p):
        return {
            "seq": lax.div(p, mps * reps),
            "mp": lax.rem(lax.div(p, reps), mps),
            "rep": lax.rem(p, reps),
        }

    weights = [
        pltpu.make_async_copy(src, dst, w_sem.at[i])
        for i, (src, dst) in enumerate(
            [
                (tokens_hbm, tokens),
                (gain_attn_hbm, gain_attn),
                (lengths_hbm, lengths),
                (w_qkv_hbm, w_qkv),
                (owner_row_hbm, owner_row),
                (gain_mlp_hbm, gain_mlp),
                (gain_final_hbm, gain_final),
                (w_colbert_hbm, w_colbert),
                (w_out_hbm, w_out),
                (w_in_hbm, w_in),
                (w_gate_hbm, w_gate),
                (w_down_hbm, w_down),
            ]
        )
    ]
    for copy in weights:
        copy.start()

    barrier = pltpu.get_barrier_semaphore()

    @pl.loop(1, peers)
    def _(k):
        pl.semaphore_signal(
            barrier, inc=1, device_id=device(lax.rem(me + k, peers)), device_id_type=MESH
        )

    def mp_copy(src, dst, send, recv, k):
        return pltpu.make_async_remote_copy(
            src_ref=src,
            dst_ref=dst,
            send_sem=send,
            recv_sem=recv,
            device_id={"mp": lax.rem(mp + k, mps)},
            device_id_type=MESH,
        )

    def chunk_row(owner, c):
        last = lax.div(owner, mps - 1)
        return pl.multiple_of((c + last * (chunks - 1 - 2 * c)) * CHUNK, CHUNK)

    def ag1(owner, c, k):
        at = pl.ds(pl.multiple_of(owner * rows + chunk_row(owner, c), CHUNK), CHUNK)
        return mp_copy(xn.at[at], xn.at[at], ag1_s.at[k - 1, c], ag1_r.at[k - 1, c], k)

    for copy in weights[:2]:
        copy.wait()

    for c in range(chunks):
        at = chunk_row(mp, c)
        part = layer_norm(tokens[pl.ds(at, CHUNK), :].astype(f32), gain_attn[...])
        xn[pl.ds(pl.multiple_of(mp * rows + at, CHUNK), CHUNK), :] = part.astype(bf16)
        if c == 0:
            pl.semaphore_wait(barrier, peers - 1)
        for k in range(1, mps):
            ag1(mp, c, k).start()

    weights[2].wait()
    docs = lengths.shape[1]
    starts = [jnp.int32(0)]
    for d in range(docs):
        starts.append(starts[-1] + lengths[0, d])

    def doc_bounds(position):
        low = jnp.zeros_like(position)
        high = jnp.zeros_like(position) + starts[1]
        for d in range(1, docs):
            inside = position >= starts[d]
            low = jnp.where(inside, starts[d], low)
            high = jnp.where(inside, starts[d + 1], high)
        return low, high

    lane = lax.broadcasted_iota(jnp.int32, (1, LANES), 1)
    first_half = lax.rem(lane, HEAD_DIM) < HEAD_DIM // 2
    frequency = jnp.exp(
        lax.rem(lane, HEAD_DIM // 2).astype(f32) * (-2.0 * LOG_BASE / HEAD_DIM)
    )

    @pl.loop(0, span // CHUNK)
    def _(i):
        at = pl.ds(pl.multiple_of(i * CHUNK, CHUNK), CHUNK)
        position = first_row + i * CHUNK + lax.broadcasted_iota(jnp.int32, (CHUNK, 1), 0)
        offset = position - doc_bounds(position)[0]
        angle = offset.astype(f32) * frequency
        cosine[at, :] = jnp.cos(angle)
        turned = jnp.sin(angle)
        sine[at, :] = jnp.where(first_half, -turned, turned)

    def rotate(values, c, s):
        swapped = jnp.where(
            first_half,
            pltpu.roll(values, LANES - HEAD_DIM // 2, 1),
            pltpu.roll(values, HEAD_DIM // 2, 1),
        )
        return values * c + swapped * s

    weights[3].wait()

    def project(x, part, c, s, put):
        for low in range(0, inner, COLS):
            y = dot(x, w_qkv[part, :, low : low + COLS])
            for half in range(0, COLS, LANES):
                piece = y[:, half : half + LANES]
                if part < 2:
                    piece = rotate(piece, c, s)
                if part == 0:
                    piece = piece * HEAD_DIM**-0.5
                put(low + half, piece.astype(bf16))

    for k in range(1, mps):
        ag1(lax.rem(mp + mps - k, mps), 0, k).wait_recv()
    top = span - WIN
    x_edge = jnp.concatenate([xn[0:WIN, :], xn[top:span, :]], axis=0)
    c_edge = jnp.concatenate([cosine[0:WIN, :], cosine[top:span, :]], axis=0)
    s_edge = jnp.concatenate([sine[0:WIN, :], sine[top:span, :]], axis=0)
    for part in (1, 2):

        def put_edge(col, piece, base=(part - 1) * inner):
            edge[:, base + col : base + col + LANES] = piece

        project(x_edge, part, c_edge, s_edge, put_edge)

    def halo(side):
        src = edge.at[pl.ds(side * WIN, WIN), :]
        dst = qkv.at[pl.ds((WIN + span) * (1 - side), WIN), pl.ds(inner, 2 * inner)]
        to = lax.rem(seq + (seqs - 1 if side == 0 else 1), seqs)
        return pltpu.make_async_remote_copy(
            src_ref=src,
            dst_ref=dst,
            send_sem=halo_s.at[side],
            recv_sem=halo_r.at[side],
            device_id={"seq": to},
            device_id_type=MESH,
        )

    @pl.when(seq > 0)
    def _():
        halo(0).start()

    @pl.when(seq < seqs - 1)
    def _():
        halo(1).start()

    @pl.when(seq == 0)
    def _():
        qkv[0:WIN, inner:] = jnp.zeros((WIN, 2 * inner), bf16)

    @pl.when(seq == seqs - 1)
    def _():
        qkv[WIN + span :, inner:] = jnp.zeros((WIN, 2 * inner), bf16)

    @pl.loop(0, mps)
    def _(i):
        owner = lax.rem(mp + mps - i, mps)

        @pl.when(i > 0)
        def _():
            for c in range(1, chunks):
                at = pl.ds(pl.multiple_of(owner * rows + chunk_row(owner, c), CHUNK), CHUNK)
                mp_copy(
                    xn.at[at], xn.at[at], ag1_s.at[i - 1, c], ag1_r.at[i - 1, c], i
                ).wait_recv()

        at = pl.multiple_of(owner * rows, rows)
        x = xn[pl.ds(at, rows), :]
        c, s = cosine[pl.ds(at, rows), :], sine[pl.ds(at, rows), :]
        for part in range(3):

            def put(col, piece, base=part * inner):
                qkv[pl.ds(pl.multiple_of(at + WIN, WIN), rows), base + col : base + col + LANES] = piece

            project(x, part, c, s, put)

    for copy in weights[4:8]:
        copy.wait()
    owner_of = owner_row[...]
    chosen = (owner_of == lax.broadcasted_iota(jnp.int32, (peers, rows), 0)).astype(f32)
    before = (
        lax.broadcasted_iota(jnp.int32, (rows, rows), 0)
        <= lax.broadcasted_iota(jnp.int32, (rows, rows), 1)
    ).astype(f32)
    running = dot(chosen.astype(bf16), before.astype(bf16))
    rank = jnp.sum(running * chosen, axis=0, keepdims=True) - 1.0
    target = owner_of.astype(f32) * slots + rank
    slot_id = lax.broadcasted_iota(jnp.int32, (peers * slots, rows), 0).astype(f32)
    disp[...] = (target == slot_id).astype(f32).astype(bf16)

    weights[8].wait()

    @pl.when(seq < seqs - 1)
    def _():
        halo(0).wait_recv()

    @pl.when(seq > 0)
    def _():
        halo(1).wait_recv()

    head_lane = lane < HEAD_DIM
    ones = jnp.ones((BLOCK + 2 * WIN, LANES), bf16)

    def attend(low):
        position = first_row + low + lax.broadcasted_iota(jnp.int32, (BLOCK, 1), 0)
        start, end = doc_bounds(position)
        start = jnp.maximum(start, position - WIN)
        end = jnp.minimum(end - 1, position + WIN)
        key = first_row + low - WIN + lax.broadcasted_iota(jnp.int32, (1, BLOCK + 2 * WIN), 1)
        allowed = (key >= start) & (key <= end)
        allowed = jnp.concatenate([allowed.astype(f32)] * 2, axis=0) > 0.5
        at_q = pl.ds(pl.multiple_of(low + WIN, WIN), BLOCK)
        at_k = pl.ds(pl.multiple_of(low, WIN), BLOCK + 2 * WIN)
        for pair in range(pairs):
            col = pair * LANES
            q = qkv[at_q, col : col + LANES].astype(f32)
            q = jnp.concatenate(
                [jnp.where(head_lane, q, 0.0), jnp.where(head_lane, 0.0, q)], axis=0
            ).astype(bf16)
            scores = dot_nt(q, qkv[at_k, inner + col : inner + col + LANES])
            scores = jnp.where(allowed, scores, -jnp.inf)
            weight = jnp.exp(scores - jnp.max(scores, axis=1, keepdims=True)).astype(bf16)
            v = qkv[at_k, 2 * inner + col : 2 * inner + col + LANES]
            o = dot(weight, jnp.concatenate([v, ones], axis=1))
            o = o[:, :LANES] / o[:, LANES:]
            ctx[:, col : col + LANES] = jnp.where(head_lane, o[:BLOCK], o[BLOCK:]).astype(bf16)
        return dot(ctx[...], w_out[...])

    def spread(buffer_s, buffer_r, send, recv, k, b):
        at = pl.ds(pl.multiple_of(b * BLOCK, BLOCK), BLOCK)
        return mp_copy(
            buffer_s.at[k - 1, at], buffer_r.at[k - 1, at], send.at[k - 1, b], recv.at[k - 1, b], k
        )

    @pl.loop(0, mps * blocks)
    def _(i):
        k = 1 + lax.rem(i, mps - 1) if mps > 2 else 1
        b = lax.div(i, mps - 1)
        is_own = i >= (mps - 1) * blocks
        own_b = i - (mps - 1) * blocks
        owner = jnp.where(is_own, mp, lax.rem(mp + k, mps))
        b = jnp.where(is_own, own_b, b)
        partial = attend(owner * rows + b * BLOCK)
        at = pl.ds(pl.multiple_of(b * BLOCK, BLOCK), BLOCK)

        @pl.when(is_own)
        def _():
            mixed[at, :] = partial + tokens[at, :].astype(f32)

        @pl.when(jnp.logical_not(is_own))
        def _():
            rs1s[k - 1, at, :] = partial.astype(bf16)
            spread(rs1s, rs1r, rs1_ss, rs1_rs, k, b).start()

    def ag2(owner, b, k):
        at = pl.ds(pl.multiple_of(owner * rows + b * BLOCK, BLOCK), BLOCK)
        return mp_copy(xn2.at[at], xn2.at[at], ag2_s.at[k - 1, b], ag2_r.at[k - 1, b], k)

    for b in range(blocks):
        at = slice(b * BLOCK, (b + 1) * BLOCK)
        value = mixed[at, :]
        for k in range(1, mps):
            spread(rs1s, rs1r, rs1_ss, rs1_rs, k, b).wait_recv()
            value = value + rs1r[k - 1, at, :].astype(f32)
        mixed[at, :] = value
        low = pl.multiple_of(mp * rows + b * BLOCK, BLOCK)
        xn2[pl.ds(low, BLOCK), :] = layer_norm(value, gain_mlp[...]).astype(bf16)
        for k in range(1, mps):
            ag2(mp, b, k).start()

    for copy in weights[9:]:
        copy.wait()

    def mlp(low):
        x = xn2[pl.ds(pl.multiple_of(low, BLOCK), BLOCK), :]
        for at in range(0, hidden, COLS):
            to = min(at + COLS, hidden)
            a = dot_nt(x, w_in[at:to, :])
            g = dot_nt(x, w_gate[at:to, :])
            a = 0.5 * a * (1.0 + lax.erf(a * (0.5**0.5)))
            hid[:, at:to] = (a * g).astype(bf16)
        return dot(hid[...], w_down[...])

    others = (mps - 1) * blocks

    @pl.loop(0, mps * blocks)
    def _(i):
        j = jnp.clip(i - 1, 0, others - 1)
        is_other = (i >= 1) & (i <= others)
        k = 1 + lax.rem(j, mps - 1) if mps > 2 else 1
        b = jnp.where(is_other, lax.div(j, mps - 1), jnp.maximum(i - others, 0))
        owner = jnp.where(is_other, lax.rem(mp + k, mps), mp)

        @pl.when(is_other)
        def _():
            back = mps - k
            at = pl.ds(pl.multiple_of(owner * rows + b * BLOCK, BLOCK), BLOCK)
            mp_copy(
                xn2.at[at], xn2.at[at], ag2_s.at[back - 1, b], ag2_r.at[back - 1, b], back
            ).wait_recv()

        partial = mlp(owner * rows + b * BLOCK)
        at = pl.ds(pl.multiple_of(b * BLOCK, BLOCK), BLOCK)

        @pl.when(is_other)
        def _():
            rs2s[k - 1, at, :] = partial.astype(bf16)
            spread(rs2s, rs2r, rs2_ss, rs2_rs, k, b).start()

        @pl.when(jnp.logical_not(is_other))
        def _():
            total[at, :] = partial + mixed[at, :]

    for b in range(blocks):
        at = slice(b * BLOCK, (b + 1) * BLOCK)
        value = total[at, :]
        for k in range(1, mps):
            spread(rs2s, rs2r, rs2_ss, rs2_rs, k, b).wait_recv()
            value = value + rs2r[k - 1, at, :].astype(f32)
        final = layer_norm(value, gain_final[...]).astype(bf16)
        raw = dot(final, w_colbert[...])
        vec[at, :] = (
            raw * lax.rsqrt(jnp.mean(raw * raw, axis=1, keepdims=True) + 1e-06)
        ).astype(bf16)

    routed = dot(disp[...], vec[...])
    for p in range(peers):
        outb[p] = routed[p * slots : (p + 1) * slots].astype(bf16)

    def a2a(to, source):
        return pltpu.make_async_remote_copy(
            src_ref=outb.at[to],
            dst_ref=out.at[source],
            send_sem=a2a_s.at[to],
            recv_sem=a2a_r.at[source],
            device_id=device(to),
            device_id_type=MESH,
        )

    @pl.loop(1, peers)
    def _(k):
        a2a(lax.rem(me + k, peers), me).start()

    own = pltpu.make_async_copy(outb.at[me], out.at[me], own_sem)
    own.start()

    for k in range(1, mps):
        for c in range(chunks):
            ag1(mp, c, k).wait_send()
        for b in range(blocks):
            spread(rs1s, rs1r, rs1_ss, rs1_rs, k, b).wait_send()
            ag2(mp, b, k).wait_send()
            spread(rs2s, rs2r, rs2_ss, rs2_rs, k, b).wait_send()

    @pl.when(seq > 0)
    def _():
        halo(0).wait_send()

    @pl.when(seq < seqs - 1)
    def _():
        halo(1).wait_send()

    own.wait()

    @pl.loop(1, peers)
    def _(k):
        other = lax.rem(me + k, peers)
        a2a(other, me).wait_send()
        a2a(other, other).wait_recv()


def per_device(
    sizes,
    tokens,
    w_qkv,
    w_attn_out,
    w_in,
    w_gate,
    w_down,
    w_colbert,
    gain_attn,
    gain_mlp,
    gain_final,
    lengths,
    owners,
):
    seqs, mps, reps = sizes
    rows, width = tokens.shape[1:]
    peers = seqs * mps * reps
    slots = max(2, 2 * rows // peers)
    inner = w_attn_out.shape[0]
    hidden = w_in.shape[1]
    span = rows * mps
    dc = w_colbert.shape[1]
    chunks, blocks = rows // CHUNK, rows // BLOCK
    anywhere = pl.BlockSpec(memory_space=pltpu.HBM)
    dma = pltpu.SemaphoreType.DMA
    return pl.pallas_call(
        functools.partial(layer_kernel, sizes),
        out_shape=jax.ShapeDtypeStruct((peers, slots, dc), bf16),
        in_specs=[anywhere] * 12,
        out_specs=anywhere,
        scratch_shapes=[
            pltpu.SMEM(lengths.shape, jnp.int32),
            pltpu.VMEM((rows, width), bf16),
            pltpu.VMEM((1, rows), jnp.int32),
            pltpu.VMEM((1, width), f32),
            pltpu.VMEM((1, width), f32),
            pltpu.VMEM((1, width), f32),
            pltpu.VMEM((width, dc), bf16),
            pltpu.VMEM((3, width, inner), bf16),
            pltpu.VMEM((inner, width), bf16),
            pltpu.VMEM((hidden, width), bf16),
            pltpu.VMEM((hidden, width), bf16),
            pltpu.VMEM((hidden, width), bf16),
            pltpu.VMEM((span, width), bf16),
            pltpu.VMEM((span, width), bf16),
            pltpu.VMEM((span + 2 * WIN, 3 * inner), bf16),
            pltpu.VMEM((2 * WIN, 2 * inner), bf16),
            pltpu.VMEM((span, LANES), f32),
            pltpu.VMEM((span, LANES), f32),
            pltpu.VMEM((peers * slots, rows), bf16),
            pltpu.VMEM((rows, width), f32),
            pltpu.VMEM((rows, width), f32),
            pltpu.VMEM((mps - 1, rows, width), bf16),
            pltpu.VMEM((mps - 1, rows, width), bf16),
            pltpu.VMEM((mps - 1, rows, width), bf16),
            pltpu.VMEM((mps - 1, rows, width), bf16),
            pltpu.VMEM((BLOCK, inner), bf16),
            pltpu.VMEM((BLOCK, hidden), bf16),
            pltpu.VMEM((rows, dc), bf16),
            pltpu.VMEM((peers, slots, dc), bf16),
            dma((12,)),
            dma((mps - 1, chunks)),
            dma((mps - 1, chunks)),
            dma((2,)),
            dma((2,)),
            dma((mps - 1, blocks)),
            dma((mps - 1, blocks)),
            dma((mps - 1, blocks)),
            dma((mps - 1, blocks)),
            dma((mps - 1, blocks)),
            dma((mps - 1, blocks)),
            dma((peers,)),
            dma((peers,)),
            dma,
        ],
        compiler_params=pltpu.CompilerParams(
            collective_id=0, has_side_effects=True, vmem_limit_bytes=60 * 1024 * 1024
        ),
    )(
        lengths,
        tokens[0],
        owners.reshape(1, rows),
        gain_attn.reshape(1, width),
        gain_mlp.reshape(1, width),
        gain_final.reshape(1, width),
        w_colbert,
        jnp.transpose(w_qkv, (1, 0, 2)),
        w_attn_out,
        w_in.T,
        w_gate.T,
        w_down.T,
    )


def solution(mesh):
    sizes = (mesh.shape["seq"], mesh.shape["mp"], mesh.shape["rep"])
    return jax.shard_map(
        functools.partial(per_device, sizes),
        mesh=mesh,
        in_specs=(
            P(("groups", "rep"), ("seq", "mp"), None),
            P(None, None, "mp"),
            P("mp", None),
            P(None, "mp"),
            P(None, "mp"),
            P(None, "mp"),
            P(),
            P(),
            P(),
            P(),
            P(("groups", "rep"), None),
            P(("groups", "rep"), ("seq", "mp"), None),
        ),
        out_specs=P(("groups", "seq", "mp", "rep"), None, None),
        check_vma=False,
    )
```

```python
import functools

import jax
import jax.numpy as jnp
from jax import lax
from jax.experimental import pallas as pl
from jax.experimental.pallas import tpu as pltpu
from jax.sharding import PartitionSpec as P

HEAD_DIM = 64
WIN = 64
LANES = 128
MESH = pl.DeviceIdType.MESH
EPS = 1e-05
LOG_BASE = 9.210340371976184

CHUNK = 128
BLOCK = 128
COLS = 256

f32 = jnp.float32
bf16 = jnp.bfloat16


def layer_norm(values, gain):
    average = jnp.mean(values, axis=-1, keepdims=True)
    centered = values - average
    spread = jnp.mean(centered * centered, axis=-1, keepdims=True)
    return centered * lax.rsqrt(spread + EPS) * gain


def dot(a, b):
    return jnp.dot(a, b, preferred_element_type=f32)


def dot_nt(a, b):
    return lax.dot_general(a, b, (((1,), (1,)), ((), ())), preferred_element_type=f32)


def layer_kernel(
    sizes,
    lengths_hbm,
    tokens_hbm,
    owner_row_hbm,
    gain_attn_hbm,
    gain_mlp_hbm,
    gain_final_hbm,
    w_colbert_hbm,
    w_qkv_hbm,
    w_out_hbm,
    w_in_hbm,
    w_gate_hbm,
    w_down_hbm,
    out,
    lengths,
    tokens,
    owner_row,
    gain_attn,
    gain_mlp,
    gain_final,
    w_colbert,
    w_qkv,
    w_out,
    w_in,
    w_gate,
    w_down,
    xn,
    xn2,
    qkv,
    edge,
    cosine,
    sine,
    disp,
    mixed,
    total,
    rs1s,
    rs1r,
    rs2s,
    rs2r,
    ctx,
    hid,
    vec,
    outb,
    w_sem,
    ag1_s,
    ag1_r,
    halo_s,
    halo_r,
    rs1_ss,
    rs1_rs,
    ag2_s,
    ag2_r,
    rs2_ss,
    rs2_rs,
    a2a_s,
    a2a_r,
    own_sem,
):
    seqs, mps, reps = sizes
    peers = seqs * mps * reps
    rows = tokens.shape[0]
    span = rows * mps
    inner = w_out.shape[0]
    pairs = inner // LANES
    hidden = w_in.shape[0]
    slots = out.shape[1]
    chunks = rows // CHUNK
    blocks = rows // BLOCK

    seq = lax.axis_index("seq")
    mp = lax.axis_index("mp")
    rep = lax.axis_index("rep")
    me = (seq * mps + mp) * reps + rep
    first_row = seq * span

    def device(p):
        return {
            "seq": lax.div(p, mps * reps),
            "mp": lax.rem(lax.div(p, reps), mps),
            "rep": lax.rem(p, reps),
        }

    weights = [
        pltpu.make_async_copy(src, dst, w_sem.at[i])
        for i, (src, dst) in enumerate(
            [
                (tokens_hbm, tokens),
                (gain_attn_hbm, gain_attn),
                (lengths_hbm, lengths),
                (w_qkv_hbm, w_qkv),
                (owner_row_hbm, owner_row),
                (gain_mlp_hbm, gain_mlp),
                (gain_final_hbm, gain_final),
                (w_colbert_hbm, w_colbert),
                (w_out_hbm, w_out),
                (w_in_hbm, w_in),
                (w_gate_hbm, w_gate),
                (w_down_hbm, w_down),
            ]
        )
    ]
    for copy in weights:
        copy.start()

    barrier = pltpu.get_barrier_semaphore()

    @pl.loop(1, peers)
    def _(k):
        pl.semaphore_signal(
            barrier, inc=1, device_id=device(lax.rem(me + k, peers)), device_id_type=MESH
        )

    def mp_copy(src, dst, send, recv, k):
        return pltpu.make_async_remote_copy(
            src_ref=src,
            dst_ref=dst,
            send_sem=send,
            recv_sem=recv,
            device_id={"mp": lax.rem(mp + k, mps)},
            device_id_type=MESH,
        )

    def chunk_row(owner, c):
        last = lax.div(owner, mps - 1)
        return pl.multiple_of((c + last * (chunks - 1 - 2 * c)) * CHUNK, CHUNK)

    def ag1(owner, c, k):
        at = pl.ds(pl.multiple_of(owner * rows + chunk_row(owner, c), CHUNK), CHUNK)
        return mp_copy(xn.at[at], xn.at[at], ag1_s.at[k - 1, c], ag1_r.at[k - 1, c], k)

    for copy in weights[:2]:
        copy.wait()

    for c in range(chunks):
        at = chunk_row(mp, c)
        part = layer_norm(tokens[pl.ds(at, CHUNK), :].astype(f32), gain_attn[...])
        xn[pl.ds(pl.multiple_of(mp * rows + at, CHUNK), CHUNK), :] = part.astype(bf16)
        if c == 0:
            pl.semaphore_wait(barrier, peers - 1)
        for k in range(1, mps):
            ag1(mp, c, k).start()

    weights[2].wait()
    docs = lengths.shape[1]
    starts = [jnp.int32(0)]
    for d in range(docs):
        starts.append(starts[-1] + lengths[0, d])

    def doc_bounds(position):
        low = jnp.zeros_like(position)
        high = jnp.zeros_like(position) + starts[1]
        for d in range(1, docs):
            inside = position >= starts[d]
            low = jnp.where(inside, starts[d], low)
            high = jnp.where(inside, starts[d + 1], high)
        return low, high

    lane = lax.broadcasted_iota(jnp.int32, (1, LANES), 1)
    first_half = lax.rem(lane, HEAD_DIM) < HEAD_DIM // 2
    frequency = jnp.exp(
        lax.rem(lane, HEAD_DIM // 2).astype(f32) * (-2.0 * LOG_BASE / HEAD_DIM)
    )

    @pl.loop(0, span // CHUNK)
    def _(i):
        at = pl.ds(pl.multiple_of(i * CHUNK, CHUNK), CHUNK)
        position = first_row + i * CHUNK + lax.broadcasted_iota(jnp.int32, (CHUNK, 1), 0)
        offset = position - doc_bounds(position)[0]
        angle = offset.astype(f32) * frequency
        cosine[at, :] = jnp.cos(angle)
        turned = jnp.sin(angle)
        sine[at, :] = jnp.where(first_half, -turned, turned)

    for copy in weights[4:8]:
        copy.wait()
    owner_of = owner_row[...]
    chosen = (owner_of == lax.broadcasted_iota(jnp.int32, (peers, rows), 0)).astype(f32)
    before = (
        lax.broadcasted_iota(jnp.int32, (rows, rows), 0)
        <= lax.broadcasted_iota(jnp.int32, (rows, rows), 1)
    ).astype(f32)
    running = dot(chosen.astype(bf16), before.astype(bf16))
    rank = jnp.sum(running * chosen, axis=0, keepdims=True) - 1.0
    target = owner_of.astype(f32) * slots + rank
    slot_id = lax.broadcasted_iota(jnp.int32, (peers * slots, rows), 0).astype(f32)
    disp[...] = (target == slot_id).astype(f32).astype(bf16)

    def rotate(values, c, s):
        swapped = jnp.where(
            first_half,
            pltpu.roll(values, LANES - HEAD_DIM // 2, 1),
            pltpu.roll(values, HEAD_DIM // 2, 1),
        )
        return values * c + swapped * s

    weights[3].wait()

    def project(x, part, c, s, put):
        for low in range(0, inner, COLS):
            y = dot(x, w_qkv[part, :, low : low + COLS])
            for half in range(0, COLS, LANES):
                piece = y[:, half : half + LANES]
                if part < 2:
                    piece = rotate(piece, c, s)
                if part == 0:
                    piece = piece * HEAD_DIM**-0.5
                put(low + half, piece.astype(bf16))

    for k in range(1, mps):
        ag1(lax.rem(mp + mps - k, mps), 0, k).wait_recv()
    top = span - WIN
    x_edge = jnp.concatenate([xn[0:WIN, :], xn[top:span, :]], axis=0)
    c_edge = jnp.concatenate([cosine[0:WIN, :], cosine[top:span, :]], axis=0)
    s_edge = jnp.concatenate([sine[0:WIN, :], sine[top:span, :]], axis=0)
    for part in (1, 2):

        def put_edge(col, piece, base=(part - 1) * inner):
            edge[:, base + col : base + col + LANES] = piece

        project(x_edge, part, c_edge, s_edge, put_edge)

    def halo(side):
        src = edge.at[pl.ds(side * WIN, WIN), :]
        dst = qkv.at[pl.ds((WIN + span) * (1 - side), WIN), pl.ds(inner, 2 * inner)]
        to = lax.rem(seq + (seqs - 1 if side == 0 else 1), seqs)
        return pltpu.make_async_remote_copy(
            src_ref=src,
            dst_ref=dst,
            send_sem=halo_s.at[side],
            recv_sem=halo_r.at[side],
            device_id={"seq": to},
            device_id_type=MESH,
        )

    @pl.when(seq > 0)
    def _():
        halo(0).start()

    @pl.when(seq < seqs - 1)
    def _():
        halo(1).start()

    @pl.when(seq == 0)
    def _():
        qkv[0:WIN, inner:] = jnp.zeros((WIN, 2 * inner), bf16)

    @pl.when(seq == seqs - 1)
    def _():
        qkv[WIN + span :, inner:] = jnp.zeros((WIN, 2 * inner), bf16)

    @pl.loop(0, mps * chunks)
    def _(j):
        i, c = lax.div(j, chunks), lax.rem(j, chunks)
        owner = lax.rem(mp + mps - i, mps)
        at = pl.multiple_of(owner * rows + chunk_row(owner, c), CHUNK)

        @pl.when((i > 0) & (c > 0))
        def _():
            chunk = xn.at[pl.ds(at, CHUNK)]
            mp_copy(chunk, chunk, ag1_s.at[i - 1, c], ag1_r.at[i - 1, c], i).wait_recv()

        x = xn[pl.ds(at, CHUNK), :]
        cos_part, sin_part = cosine[pl.ds(at, CHUNK), :], sine[pl.ds(at, CHUNK), :]
        for part in range(3):

            def put(col, piece, base=part * inner):
                qkv[pl.ds(pl.multiple_of(at + WIN, WIN), CHUNK), base + col : base + col + LANES] = piece

            project(x, part, cos_part, sin_part, put)

    weights[8].wait()

    @pl.when(seq < seqs - 1)
    def _():
        halo(0).wait_recv()

    @pl.when(seq > 0)
    def _():
        halo(1).wait_recv()

    head_lane = lane < HEAD_DIM
    ones = jnp.ones((BLOCK + 2 * WIN, LANES), bf16)

    def attend(low):
        position = first_row + low + lax.broadcasted_iota(jnp.int32, (BLOCK, 1), 0)
        start, end = doc_bounds(position)
        start = jnp.maximum(start, position - WIN)
        end = jnp.minimum(end - 1, position + WIN)
        key = first_row + low - WIN + lax.broadcasted_iota(jnp.int32, (1, BLOCK + 2 * WIN), 1)
        allowed = (key >= start) & (key <= end)
        allowed = jnp.concatenate([allowed.astype(f32)] * 2, axis=0) > 0.5
        at_q = pl.ds(pl.multiple_of(low + WIN, WIN), BLOCK)
        at_k = pl.ds(pl.multiple_of(low, WIN), BLOCK + 2 * WIN)
        for pair in range(pairs):
            col = pair * LANES
            q = qkv[at_q, col : col + LANES].astype(f32)
            q = jnp.concatenate(
                [jnp.where(head_lane, q, 0.0), jnp.where(head_lane, 0.0, q)], axis=0
            ).astype(bf16)
            scores = dot_nt(q, qkv[at_k, inner + col : inner + col + LANES])
            scores = jnp.where(allowed, scores, -jnp.inf)
            weight = jnp.exp(scores - jnp.max(scores, axis=1, keepdims=True)).astype(bf16)
            v = qkv[at_k, 2 * inner + col : 2 * inner + col + LANES]
            o = dot(weight, jnp.concatenate([v, ones], axis=1))
            o = o[:, :LANES] / o[:, LANES:]
            ctx[:, col : col + LANES] = jnp.where(head_lane, o[:BLOCK], o[BLOCK:]).astype(bf16)
        return dot(ctx[...], w_out[...])

    def spread(buffer_s, buffer_r, send, recv, k, b):
        at = pl.ds(pl.multiple_of(b * BLOCK, BLOCK), BLOCK)
        return mp_copy(
            buffer_s.at[k - 1, at], buffer_r.at[k - 1, at], send.at[k - 1, b], recv.at[k - 1, b], k
        )

    @pl.loop(0, mps * blocks)
    def _(i):
        k = 1 + lax.rem(i, mps - 1) if mps > 2 else 1
        b = lax.div(i, mps - 1)
        is_own = i >= (mps - 1) * blocks
        own_b = i - (mps - 1) * blocks
        owner = jnp.where(is_own, mp, lax.rem(mp + k, mps))
        b = jnp.where(is_own, own_b, b)
        partial = attend(owner * rows + b * BLOCK)
        at = pl.ds(pl.multiple_of(b * BLOCK, BLOCK), BLOCK)

        @pl.when(is_own)
        def _():
            mixed[at, :] = partial + tokens[at, :].astype(f32)

        @pl.when(jnp.logical_not(is_own))
        def _():
            rs1s[k - 1, at, :] = partial.astype(bf16)
            spread(rs1s, rs1r, rs1_ss, rs1_rs, k, b).start()

    def ag2(owner, b, k):
        at = pl.ds(pl.multiple_of(owner * rows + b * BLOCK, BLOCK), BLOCK)
        return mp_copy(xn2.at[at], xn2.at[at], ag2_s.at[k - 1, b], ag2_r.at[k - 1, b], k)

    for b in range(blocks):
        at = slice(b * BLOCK, (b + 1) * BLOCK)
        value = mixed[at, :]
        for k in range(1, mps):
            spread(rs1s, rs1r, rs1_ss, rs1_rs, k, b).wait_recv()
            value = value + rs1r[k - 1, at, :].astype(f32)
        mixed[at, :] = value
        low = pl.multiple_of(mp * rows + b * BLOCK, BLOCK)
        xn2[pl.ds(low, BLOCK), :] = layer_norm(value, gain_mlp[...]).astype(bf16)
        for k in range(1, mps):
            ag2(mp, b, k).start()

    for copy in weights[9:]:
        copy.wait()

    def mlp(low):
        x = xn2[pl.ds(pl.multiple_of(low, BLOCK), BLOCK), :]
        for at in range(0, hidden, COLS):
            to = min(at + COLS, hidden)
            a = dot_nt(x, w_in[at:to, :])
            g = dot_nt(x, w_gate[at:to, :])
            a = 0.5 * a * (1.0 + lax.erf(a * (0.5**0.5)))
            hid[:, at:to] = (a * g).astype(bf16)
        return dot(hid[...], w_down[...])

    others = (mps - 1) * blocks

    @pl.loop(0, mps * blocks)
    def _(i):
        j = jnp.clip(i - 1, 0, others - 1)
        is_other = (i >= 1) & (i <= others)
        k = 1 + lax.rem(j, mps - 1) if mps > 2 else 1
        b = jnp.where(is_other, lax.div(j, mps - 1), jnp.maximum(i - others, 0))
        owner = jnp.where(is_other, lax.rem(mp + k, mps), mp)

        @pl.when(is_other)
        def _():
            back = mps - k
            at = pl.ds(pl.multiple_of(owner * rows + b * BLOCK, BLOCK), BLOCK)
            mp_copy(
                xn2.at[at], xn2.at[at], ag2_s.at[back - 1, b], ag2_r.at[back - 1, b], back
            ).wait_recv()

        partial = mlp(owner * rows + b * BLOCK)
        at = pl.ds(pl.multiple_of(b * BLOCK, BLOCK), BLOCK)

        @pl.when(is_other)
        def _():
            rs2s[k - 1, at, :] = partial.astype(bf16)
            spread(rs2s, rs2r, rs2_ss, rs2_rs, k, b).start()

        @pl.when(jnp.logical_not(is_other))
        def _():
            total[at, :] = partial + mixed[at, :]

    for b in range(blocks):
        at = slice(b * BLOCK, (b + 1) * BLOCK)
        value = total[at, :]
        for k in range(1, mps):
            spread(rs2s, rs2r, rs2_ss, rs2_rs, k, b).wait_recv()
            value = value + rs2r[k - 1, at, :].astype(f32)
        final = layer_norm(value, gain_final[...]).astype(bf16)
        raw = dot(final, w_colbert[...])
        vec[at, :] = (
            raw * lax.rsqrt(jnp.mean(raw * raw, axis=1, keepdims=True) + 1e-06)
        ).astype(bf16)

    routed = dot(disp[...], vec[...])
    for p in range(peers):
        outb[p] = routed[p * slots : (p + 1) * slots].astype(bf16)

    def a2a(to, source):
        return pltpu.make_async_remote_copy(
            src_ref=outb.at[to],
            dst_ref=out.at[source],
            send_sem=a2a_s.at[to],
            recv_sem=a2a_r.at[source],
            device_id=device(to),
            device_id_type=MESH,
        )

    @pl.loop(1, peers)
    def _(k):
        a2a(lax.rem(me + k, peers), me).start()

    own = pltpu.make_async_copy(outb.at[me], out.at[me], own_sem)
    own.start()

    for k in range(1, mps):
        for c in range(chunks):
            ag1(mp, c, k).wait_send()
        for b in range(blocks):
            spread(rs1s, rs1r, rs1_ss, rs1_rs, k, b).wait_send()
            ag2(mp, b, k).wait_send()
            spread(rs2s, rs2r, rs2_ss, rs2_rs, k, b).wait_send()

    @pl.when(seq > 0)
    def _():
        halo(0).wait_send()

    @pl.when(seq < seqs - 1)
    def _():
        halo(1).wait_send()

    own.wait()

    @pl.loop(1, peers)
    def _(k):
        other = lax.rem(me + k, peers)
        a2a(other, me).wait_send()
        a2a(other, other).wait_recv()


def per_device(
    sizes,
    tokens,
    w_qkv,
    w_attn_out,
    w_in,
    w_gate,
    w_down,
    w_colbert,
    gain_attn,
    gain_mlp,
    gain_final,
    lengths,
    owners,
):
    seqs, mps, reps = sizes
    rows, width = tokens.shape[1:]
    peers = seqs * mps * reps
    slots = max(2, 2 * rows // peers)
    inner = w_attn_out.shape[0]
    hidden = w_in.shape[1]
    span = rows * mps
    dc = w_colbert.shape[1]
    chunks, blocks = rows // CHUNK, rows // BLOCK
    anywhere = pl.BlockSpec(memory_space=pltpu.HBM)
    dma = pltpu.SemaphoreType.DMA
    return pl.pallas_call(
        functools.partial(layer_kernel, sizes),
        out_shape=jax.ShapeDtypeStruct((peers, slots, dc), bf16),
        in_specs=[anywhere] * 12,
        out_specs=anywhere,
        scratch_shapes=[
            pltpu.SMEM(lengths.shape, jnp.int32),
            pltpu.VMEM((rows, width), bf16),
            pltpu.VMEM((1, rows), jnp.int32),
            pltpu.VMEM((1, width), f32),
            pltpu.VMEM((1, width), f32),
            pltpu.VMEM((1, width), f32),
            pltpu.VMEM((width, dc), bf16),
            pltpu.VMEM((3, width, inner), bf16),
            pltpu.VMEM((inner, width), bf16),
            pltpu.VMEM((hidden, width), bf16),
            pltpu.VMEM((hidden, width), bf16),
            pltpu.VMEM((hidden, width), bf16),
            pltpu.VMEM((span, width), bf16),
            pltpu.VMEM((span, width), bf16),
            pltpu.VMEM((span + 2 * WIN, 3 * inner), bf16),
            pltpu.VMEM((2 * WIN, 2 * inner), bf16),
            pltpu.VMEM((span, LANES), f32),
            pltpu.VMEM((span, LANES), f32),
            pltpu.VMEM((peers * slots, rows), bf16),
            pltpu.VMEM((rows, width), f32),
            pltpu.VMEM((rows, width), f32),
            pltpu.VMEM((mps - 1, rows, width), bf16),
            pltpu.VMEM((mps - 1, rows, width), bf16),
            pltpu.VMEM((mps - 1, rows, width), bf16),
            pltpu.VMEM((mps - 1, rows, width), bf16),
            pltpu.VMEM((BLOCK, inner), bf16),
            pltpu.VMEM((BLOCK, hidden), bf16),
            pltpu.VMEM((rows, dc), bf16),
            pltpu.VMEM((peers, slots, dc), bf16),
            dma((12,)),
            dma((mps - 1, chunks)),
            dma((mps - 1, chunks)),
            dma((2,)),
            dma((2,)),
            dma((mps - 1, blocks)),
            dma((mps - 1, blocks)),
            dma((mps - 1, blocks)),
            dma((mps - 1, blocks)),
            dma((mps - 1, blocks)),
            dma((mps - 1, blocks)),
            dma((peers,)),
            dma((peers,)),
            dma,
        ],
        compiler_params=pltpu.CompilerParams(
            collective_id=0, has_side_effects=True, vmem_limit_bytes=60 * 1024 * 1024
        ),
    )(
        lengths,
        tokens[0],
        owners.reshape(1, rows),
        gain_attn.reshape(1, width),
        gain_mlp.reshape(1, width),
        gain_final.reshape(1, width),
        w_colbert,
        jnp.transpose(w_qkv, (1, 0, 2)),
        w_attn_out,
        w_in.T,
        w_gate.T,
        w_down.T,
    )


def solution(mesh):
    sizes = (mesh.shape["seq"], mesh.shape["mp"], mesh.shape["rep"])
    return jax.shard_map(
        functools.partial(per_device, sizes),
        mesh=mesh,
        in_specs=(
            P(("groups", "rep"), ("seq", "mp"), None),
            P(None, None, "mp"),
            P("mp", None),
            P(None, "mp"),
            P(None, "mp"),
            P(None, "mp"),
            P(),
            P(),
            P(),
            P(),
            P(("groups", "rep"), None),
            P(("groups", "rep"), ("seq", "mp"), None),
        ),
        out_specs=P(("groups", "seq", "mp", "rep"), None, None),
        check_vma=False,
    )
```
